256 devices in a mesh: ta: 32 (over y, z), gz: 8 (over x, core).
Axes of the slice: x: 4, y: 4, z: 8, core: 2. Of those that a mesh axis runs over, the one named last changes fastest.
Arguments:
- level2_residual: bfloat16 [32, 8, 3, 4, 48, 1536], P('ta', 'gz'), may hold values from -6 to 6
- prolongator: bfloat16 [32, 8, 3, 4, 1536, 128], P('ta', 'gz'), may hold values from -0.15625 to 0.15625
- coarse_links: bfloat16 [9, 32, 8, 3, 4, 128, 128], P(None, 'ta', 'gz'), may hold values from -0.15625 to 0.15625
Outputs:
- correction: bfloat16 [32, 8, 3, 4, 48, 1536], P('ta', 'gz')
The draws below stay inside these ranges and needn't reach their ends.
All inputs are finite; a program needn't handle non-finite values.
Results may differ from the reference program's by a relative error of at most 0.034.
Values may be sent and summed in bfloat16 or wider, within the bound.
No kernel may reach another device: no remote copies, remote signals or barrier semaphores. Data moves between devices by JAX's collectives and lax.ppermute only.
A program may use at most 64 MiB of HBM per device.

```python
import jax
import jax.numpy as jnp
from jax import lax

K2 = 96
K3 = 128
BLOCK = 16
RHS = 48
ITERS = 16
Y3 = 3
X3 = 4
NT3 = 32
NZ3 = 8


def shard_levels(stream_key, extent, pieces, smallest, top_value):
    gain, own = 1.0, jax.random.fold_in(stream_key, 6)
    for dim, blocks in pieces:
        steps = jnp.exp(jax.random.uniform(jax.random.fold_in(own, dim), (blocks,), jnp.float32, smallest / len(pieces), top_value / len(pieces)))
        gain = gain * jnp.repeat(steps, extent[dim] // blocks).reshape([-1 if axis == dim else 1 for axis in range(len(extent))])
    return gain


def centred(own_key, dims, width, most, cuts=(), held_as=jnp.bfloat16):
    gain = shard_levels(own_key, dims, cuts, -0.22, 0.18) if cuts else 1.0
    result = jax.random.normal(own_key, dims, jnp.float32) * width * gain
    return jnp.minimum(jnp.maximum(result, -most), most).astype(held_as)


def setup_inputs(seed: int = 0) -> dict:
    splits = jax.random.split(jax.random.key(seed), 4)
    level2_residual = centred(splits[0], (NT3, NZ3, Y3, X3, RHS, BLOCK * K2), 1.0, 6.0, ((0, 32), (1, 8)))
    prolongator = centred(splits[1], (NT3, NZ3, Y3, X3, BLOCK * K2, K3), (BLOCK * K2) ** -0.5, 0.15625, ((0, 32), (1, 8)))
    coarse_links = centred(splits[2], (9, NT3, NZ3, Y3, X3, K3, K3), (11 * K3) ** -0.5, 0.15625, ((1, 32), (2, 8)))
    return dict(level2_residual=level2_residual, prolongator=prolongator, coarse_links=coarse_links)


def neighbours(source):
    return [source,
            jnp.roll(source, -1, 3), jnp.roll(source, 1, 3),
            jnp.roll(source, -1, 2), jnp.roll(source, 1, 2),
            jnp.roll(source, -1, 1), jnp.roll(source, 1, 1),
            jnp.concatenate([source[1:], -source[:1]], 0),
            jnp.concatenate([-source[-1:], source[:-1]], 0)]


def stencil(coarse_links, rounded):
    source = rounded.astype(jnp.float32)
    summed = jnp.zeros(source.shape, jnp.float32)
    for direction, shifted in enumerate(neighbours(source)):
        summed = summed + jnp.einsum('tzyxok,tzyxrk->tzyxro', coarse_links[direction].astype(jnp.float32), shifted, precision=lax.Precision.HIGHEST)
    return summed


def restrict_time(operands):
    residual_slice, prolong_slice = operands
    return jnp.einsum('zyxrj,zyxjk->zyxrk', residual_slice.astype(jnp.float32), prolong_slice.astype(jnp.float32), precision=lax.Precision.HIGHEST)


def prolong_time(operands):
    iterate_slice, prolong_slice = operands
    return jnp.einsum('zyxrk,zyxjk->zyxrj', iterate_slice.astype(jnp.float32), prolong_slice.astype(jnp.float32), precision=lax.Precision.HIGHEST)


def reference(level2_residual, prolongator, coarse_links):
    coarse_rhs = lax.map(restrict_time, (level2_residual, prolongator)).astype(jnp.bfloat16)
    target = coarse_rhs.astype(jnp.float32)

    def sweep(sweep_index, iterate):
        rounded = lax.optimization_barrier(iterate.astype(jnp.bfloat16))
        return target - stencil(coarse_links, rounded)

    iterate = lax.fori_loop(0, ITERS, sweep, target)
    settled = iterate.astype(jnp.bfloat16)
    return lax.map(prolong_time, (settled, prolongator)).astype(jnp.bfloat16)
```

```python
import functools

import jax
import jax.numpy as jnp
from jax import lax
from jax.experimental import pallas as pl
from jax.experimental.pallas import tpu as pltpu
from jax.sharding import PartitionSpec as P

ITERS = 16
LIMIT = 40 * 2**20
VMEM = pl.BlockSpec(memory_space=pltpu.VMEM)
HBM = pl.BlockSpec(memory_space=pltpu.HBM)
SMEM = pl.BlockSpec(memory_space=pltpu.SMEM)
NN = (((1,), (0,)), ((), ()))


def call(kernel, ins, outs, scratch=(), in_specs=None, out_specs=None, flops=0, touched=0):
    in_specs = in_specs or [VMEM] * len(ins)
    out_specs = out_specs or [VMEM] * len(outs)
    ins = [
        x if spec is SMEM else pltpu.with_memory_space_constraint(x, spec.memory_space)
        for x, spec in zip(ins, in_specs)
    ]
    return pl.pallas_call(
        kernel,
        in_specs=in_specs,
        out_specs=out_specs,
        out_shape=[
            pltpu.VMEM(o.shape, o.dtype) if spec is VMEM else o for o, spec in zip(outs, out_specs)
        ],
        scratch_shapes=list(scratch),
        compiler_params=pltpu.CompilerParams(vmem_limit_bytes=LIMIT),
        cost_estimate=pl.CostEstimate(flops=flops, bytes_accessed=touched, transcendentals=0),
    )(*ins)


def shape(dims, dtype=jnp.bfloat16):
    return jax.ShapeDtypeStruct(dims, dtype)


def dot(a, b):
    return lax.dot_general(a, b, NN, preferred_element_type=jnp.float32)


def restrict_kernel(residual, prolongator, rhs, held, buffer, sems):
    sites = rhs.shape[0]
    copies = []
    for s in range(sites):
        copies.append(
            (
                pltpu.make_async_copy(residual.at[s], buffer.at[s], sems.at[0, s]),
                pltpu.make_async_copy(prolongator.at[s], held.at[s], sems.at[1, s]),
            )
        )
        for c in copies[-1]:
            c.start()
    for s in range(sites):
        for c in copies[s]:
            c.wait()
        rhs[s] = dot(buffer[s], held[s]).astype(rhs.dtype)


def links_kernel(slots, links, local, remote):
    sites = local.shape[0]
    wide = links.shape[-1]
    for i in range(9):
        source = i if i < 5 else slots[i - 5]
        for s in range(sites):
            block = links[source, s].T
            if i < 5:
                local[s, i * wide : (i + 1) * wide, :] = block
            else:
                if i == 5:
                    block = block * slots[4].astype(block.dtype)
                remote[s, (i - 5) * wide : (i - 4) * wide, :] = block


def local_kernel(ny, nx, rhs, value, weights, out):
    for y in range(ny):
        for x in range(nx):
            s = y * nx + x
            near = [
                s,
                y * nx + (x + 1) % nx,
                y * nx + (x - 1) % nx,
                (y + 1) % ny * nx + x,
                (y - 1) % ny * nx + x,
            ]
            lhs = jnp.concatenate([value[n] for n in near], 1)
            out[s] = rhs[s].astype(jnp.float32) - dot(lhs, weights[s])


def remote_kernel(part, a, b, c, d, weights, out):
    for s in range(part.shape[0]):
        lhs = jnp.concatenate([a[s], b[s], c[s], d[s]], 1)
        out[s] = (part[s] - dot(lhs, weights[s])).astype(out.dtype)


def transpose_kernel(held, out):
    for s in range(held.shape[0]):
        out[s] = held[s].T


def prolong_kernel(value, weights, out, buffer, sems):
    copies = []
    for s in range(value.shape[0]):
        buffer[s] = dot(value[s], weights[s]).astype(buffer.dtype)
        copies.append(pltpu.make_async_copy(buffer.at[s], out.at[s], sems.at[s]))
        copies[-1].start()
    for c in copies:
        c.wait()


def swap(count, first):
    pairs = [((i + first) % count, (i + first + 1) % count) for i in range(0, count, 2)]
    return pairs + [(b, a) for a, b in pairs]


def per_device(level2_residual, prolongator, coarse_links):
    nt, nz = lax.axis_size("ta"), lax.axis_size("gz")
    t, z = lax.axis_index("ta"), lax.axis_index("gz")
    ny, nx, rhs_count, fine = level2_residual.shape[2:]
    wide = prolongator.shape[-1]
    sites = ny * nx
    residual = level2_residual.reshape(sites, rhs_count, fine)
    prolong = prolongator.reshape(sites, fine, wide)
    links = coarse_links.reshape(9, sites, wide, wide)
    field = (sites, rhs_count, wide)
    flops = 2 * sites * rhs_count * wide * wide

    rhs, held = call(
        restrict_kernel,
        [residual, prolong],
        [shape(field), shape(prolong.shape)],
        [pltpu.VMEM(residual.shape, residual.dtype), pltpu.SemaphoreType.DMA((2, sites))],
        in_specs=[HBM, HBM],
    )
    t_odd, z_odd = t % 2, z % 2
    edge = (t == 0) | (t == nt - 1)
    slots = jnp.stack([8 - t_odd, 7 + t_odd, 6 - z_odd, 5 + z_odd, jnp.where(edge, -1, 1)]).astype(
        jnp.int32
    )
    local_weights, remote_weights = call(
        links_kernel,
        [slots, links],
        [shape((sites, 5 * wide, wide)), shape((sites, 4 * wide, wide))],
        in_specs=[SMEM, VMEM],
    )

    value = rhs
    for _ in range(ITERS):
        z_near = lax.ppermute(value, "gz", swap(nz, 0))
        z_far = lax.ppermute(value, "gz", swap(nz, 1))
        t_near = lax.ppermute(value, "ta", swap(nt, 0))
        t_far = lax.ppermute(value, "ta", swap(nt, 1))
        (part,) = call(
            functools.partial(local_kernel, ny, nx),
            [rhs, value, local_weights],
            [shape(field, jnp.float32)],
            flops=5 * flops,
        )
        (value,) = call(
            remote_kernel,
            [part, t_far, t_near, z_far, z_near, remote_weights],
            [shape(field)],
            flops=4 * flops,
        )

    (weights,) = call(transpose_kernel, [held], [shape((sites, wide, fine))])
    (out,) = call(
        prolong_kernel,
        [value, weights],
        [shape((sites, rhs_count, fine))],
        [pltpu.VMEM((sites, rhs_count, fine), jnp.bfloat16), pltpu.SemaphoreType.DMA((sites,))],
        out_specs=[HBM],
    )
    return out.reshape(level2_residual.shape)


def solution(mesh):
    placed = (
        P("ta", "gz", None, None, None, None),
        P("ta", "gz", None, None, None, None),
        P(None, "ta", "gz", None, None, None, None),
    )
    return jax.shard_map(
        per_device,
        mesh=mesh,
        in_specs=placed,
        out_specs=P("ta", "gz", None, None, None, None),
        check_vma=False,
    )
```

```python
import functools

import jax
import jax.numpy as jnp
from jax import lax
from jax.experimental import pallas as pl
from jax.experimental.pallas import tpu as pltpu
from jax.sharding import PartitionSpec as P

ITERS = 16
LIMIT = 40 * 2**20
VMEM = pl.BlockSpec(memory_space=pltpu.VMEM)
HBM = pl.BlockSpec(memory_space=pltpu.HBM)
SMEM = pl.BlockSpec(memory_space=pltpu.SMEM)
NN = (((1,), (0,)), ((), ()))


def call(kernel, ins, outs, scratch=(), in_specs=None, out_specs=None, flops=0, aliases=None):
    in_specs = in_specs or [VMEM] * len(ins)
    out_specs = out_specs or [VMEM] * len(outs)
    ins = [
        x if spec is SMEM else pltpu.with_memory_space_constraint(x, spec.memory_space)
        for x, spec in zip(ins, in_specs)
    ]
    return pl.pallas_call(
        kernel,
        in_specs=in_specs,
        out_specs=out_specs,
        out_shape=[
            pltpu.VMEM(o.shape, o.dtype) if spec is VMEM else o for o, spec in zip(outs, out_specs)
        ],
        scratch_shapes=list(scratch),
        compiler_params=pltpu.CompilerParams(vmem_limit_bytes=LIMIT),
        input_output_aliases=aliases or {},
        cost_estimate=pl.CostEstimate(flops=flops, bytes_accessed=0, transcendentals=0),
    )(*ins)


def shape(dims, dtype=jnp.bfloat16):
    return jax.ShapeDtypeStruct(dims, dtype)


def dot(a, b):
    return lax.dot_general(a, b, NN, preferred_element_type=jnp.float32)


def restrict_kernel(residual, prolongator, rhs, buffer, held, sems):
    sites = rhs.shape[0]
    copies = []
    for s in range(sites):
        copies.append(
            (
                pltpu.make_async_copy(residual.at[s], buffer.at[s], sems.at[0, s]),
                pltpu.make_async_copy(prolongator.at[s], held.at[s], sems.at[1, s]),
            )
        )
        for c in copies[-1]:
            c.start()
    for s in range(sites):
        for c in copies[s]:
            c.wait()
        rhs[s] = dot(buffer[s], held[s]).astype(rhs.dtype)


def links_kernel(slots, links, local, remote, buffer, sems):
    sites = local.shape[0]
    wide = links.shape[-1]
    copies = []
    for i in range(9):
        source = i if i < 5 else slots[i - 5]
        copies.append(pltpu.make_async_copy(links.at[source], buffer.at[i], sems.at[i]))
        copies[-1].start()
    for i in range(9):
        copies[i].wait()
        for s in range(sites):
            block = buffer[i, s].T
            if i < 5:
                local[s, i * wide : (i + 1) * wide, :] = block
            else:
                if i == 5:
                    block = block * slots[4].astype(block.dtype)
                remote[s, (i - 5) * wide : (i - 4) * wide, :] = block


def local_kernel(ny, nx, rhs, value, weights, out):
    for y in range(ny):
        for x in range(nx):
            s = y * nx + x
            near = [
                s,
                y * nx + (x + 1) % nx,
                y * nx + (x - 1) % nx,
                (y + 1) % ny * nx + x,
                (y - 1) % ny * nx + x,
            ]
            lhs = jnp.concatenate([value[n] for n in near], 1)
            out[s] = rhs[s].astype(jnp.float32) - dot(lhs, weights[s])


def remote_kernel(part, a, b, c, d, weights, out):
    for s in range(part.shape[0]):
        lhs = jnp.concatenate([a[s], b[s], c[s], d[s]], 1)
        out[s] = (part[s] - dot(lhs, weights[s])).astype(out.dtype)


def after_kernel(part, arrived, out):
    pass


def transpose_kernel(held, out):
    for s in range(held.shape[0]):
        out[s] = held[s].T


def prolong_kernel(value, weights, out, buffer, sems):
    copies = []
    for s in range(value.shape[0]):
        buffer[s] = dot(value[s], weights[s]).astype(buffer.dtype)
        copies.append(pltpu.make_async_copy(buffer.at[s], out.at[s], sems.at[s]))
        copies[-1].start()
    for c in copies:
        c.wait()


def swap(count, first):
    pairs = [((i + first) % count, (i + first + 1) % count) for i in range(0, count, 2)]
    return pairs + [(b, a) for a, b in pairs]


def per_device(level2_residual, prolongator, coarse_links):
    nt, nz = lax.axis_size("ta"), lax.axis_size("gz")
    t, z = lax.axis_index("ta"), lax.axis_index("gz")
    ny, nx, rhs_count, fine = level2_residual.shape[2:]
    wide = prolongator.shape[-1]
    sites = ny * nx
    residual = level2_residual.reshape(sites, rhs_count, fine)
    prolong = prolongator.reshape(sites, fine, wide)
    links = coarse_links.reshape(9, sites, wide, wide)
    field = (sites, rhs_count, wide)
    flops = 2 * sites * rhs_count * wide * wide

    (rhs,) = call(
        restrict_kernel,
        [residual, prolong],
        [shape(field)],
        [
            pltpu.VMEM(residual.shape, residual.dtype),
            pltpu.VMEM(prolong.shape, prolong.dtype),
            pltpu.SemaphoreType.DMA((2, sites)),
        ],
        in_specs=[HBM, HBM],
    )
    t_odd, z_odd = t % 2, z % 2
    edge = (t == 0) | (t == nt - 1)
    slots = jnp.stack([8 - t_odd, 7 + t_odd, 6 - z_odd, 5 + z_odd, jnp.where(edge, -1, 1)]).astype(
        jnp.int32
    )
    local_weights, remote_weights = call(
        links_kernel,
        [slots, links],
        [shape((sites, 5 * wide, wide)), shape((sites, 4 * wide, wide))],
        [pltpu.VMEM(links.shape, links.dtype), pltpu.SemaphoreType.DMA((9,))],
        in_specs=[SMEM, HBM],
    )

    def sweep(_, value):
        z_near = lax.ppermute(value, "gz", swap(nz, 0))
        z_far = lax.ppermute(value, "gz", swap(nz, 1))
        t_near = lax.ppermute(value, "ta", swap(nt, 0))
        t_far = lax.ppermute(value, "ta", swap(nt, 1))
        (part,) = call(
            functools.partial(local_kernel, ny, nx),
            [rhs, value, local_weights],
            [shape(field, jnp.float32)],
            flops=5 * flops,
        )
        for arrived in (t_far, t_near, z_far):
            (part,) = call(
                after_kernel, [part, arrived], [shape(field, jnp.float32)], aliases={0: 0}
            )
        (value,) = call(
            remote_kernel,
            [part, t_far, t_near, z_far, z_near, remote_weights],
            [shape(field)],
            flops=4 * flops,
        )
        return value

    value = sweep(0, rhs)
    value = lax.fori_loop(1, ITERS - 1, sweep, value)
    value = sweep(ITERS - 1, value)

    (weights,) = call(transpose_kernel, [prolong], [shape((sites, wide, fine))])
    (out,) = call(
        prolong_kernel,
        [value, weights],
        [shape((sites, rhs_count, fine))],
        [pltpu.VMEM((sites, rhs_count, fine), jnp.bfloat16), pltpu.SemaphoreType.DMA((sites,))],
        out_specs=[HBM],
    )
    return out.reshape(level2_residual.shape)


def solution(mesh):
    placed = (
        P("ta", "gz", None, None, None, None),
        P("ta", "gz", None, None, None, None),
        P(None, "ta", "gz", None, None, None, None),
    )
    return jax.shard_map(
        per_device,
        mesh=mesh,
        in_specs=placed,
        out_specs=P("ta", "gz", None, None, None, None),
        check_vma=False,
    )
```

```python
import functools

import jax
import jax.numpy as jnp
from jax import lax
from jax.experimental import pallas as pl
from jax.experimental.pallas import tpu as pltpu
from jax.sharding import PartitionSpec as P

ITERS = 16
LIMIT = 16 * 2**20
VMEM = pl.BlockSpec(memory_space=pltpu.VMEM)
HBM = pl.BlockSpec(memory_space=pltpu.HBM)
SMEM = pl.BlockSpec(memory_space=pltpu.SMEM)
NN = (((1,), (0,)), ((), ()))


def call(kernel, ins, outs, scratch=(), in_specs=None, out_specs=None, flops=0):
    in_specs = in_specs or [VMEM] * len(ins)
    out_specs = out_specs or [VMEM] * len(outs)
    ins = [
        x if spec is SMEM else pltpu.with_memory_space_constraint(x, spec.memory_space)
        for x, spec in zip(ins, in_specs)
    ]
    return pl.pallas_call(
        kernel,
        in_specs=in_specs,
        out_specs=out_specs,
        out_shape=[
            pltpu.VMEM(o.shape, o.dtype) if spec is VMEM else o for o, spec in zip(outs, out_specs)
        ],
        scratch_shapes=list(scratch),
        compiler_params=pltpu.CompilerParams(vmem_limit_bytes=LIMIT),
        cost_estimate=pl.CostEstimate(flops=flops, bytes_accessed=0, transcendentals=0),
    )(*ins)


def shape(dims, dtype=jnp.bfloat16):
    return jax.ShapeDtypeStruct(dims, dtype)


def dot(a, b):
    return lax.dot_general(a, b, NN, preferred_element_type=jnp.float32)


def restrict_kernel(residual, prolongator, rhs, buffer, held, sems):
    sites = rhs.shape[0]
    copies = []
    for s in range(sites):
        copies.append(
            (
                pltpu.make_async_copy(residual.at[s], buffer.at[s], sems.at[0, s]),
                pltpu.make_async_copy(prolongator.at[s], held.at[s], sems.at[1, s]),
            )
        )
        for c in copies[-1]:
            c.start()
    for s in range(sites):
        for c in copies[s]:
            c.wait()
        rhs[s] = dot(buffer[s], held[s]).astype(rhs.dtype)


def links_kernel(slots, links, local, remote, buffer, sems):
    sites = local.shape[0]
    wide = links.shape[-1]
    def fetch(i):
        source = i if i < 5 else slots[i - 5]
        return pltpu.make_async_copy(links.at[source], buffer.at[i], sems.at[i])

    for i in range(9):
        fetch(i).start()

    def turn(first, out, i, _):
        pltpu.make_async_copy(links.at[0], buffer.at[first + i], sems.at[first + i]).wait()
        rows = pl.ds(pl.multiple_of(i * wide, wide), wide)
        for s in range(sites):
            out[s, rows, :] = buffer[first + i, s].T
        return 0

    lax.fori_loop(0, 5, functools.partial(turn, 0, local), 0)
    lax.fori_loop(0, 4, functools.partial(turn, 5, remote), 0)

    @pl.when(slots[4] < 0)
    def _():
        remote[:, :wide, :] = -remote[:, :wide, :]


def local_kernel(ny, nx, rhs, value, weights, out):

    def row(y, _):
        above, below = lax.rem(y + 1, ny), lax.rem(y + ny - 1, ny)
        for x in range(nx):
            s = y * nx + x
            near = [s, y * nx + (x + 1) % nx, y * nx + (x - 1) % nx, above * nx + x, below * nx + x]
            lhs = jnp.concatenate([value[n] for n in near], 1)
            out[s] = rhs[s].astype(jnp.float32) - dot(lhs, weights[s])
        return 0

    lax.fori_loop(0, ny, row, 0)


def remote_kernel(part, a, b, c, d, weights, token, out):
    for s in range(part.shape[0]):
        lhs = jnp.concatenate([a[s], b[s], c[s], d[s]], 1)
        out[s] = (part[s] - dot(lhs, weights[s])).astype(out.dtype)


def after_kernel(earlier, arrived, token):
    token[...] = jnp.zeros_like(token)


def transpose_kernel(prolongator, earlier, out, buffer, sems):
    sites = out.shape[0]

    def fetch(s):
        return pltpu.make_async_copy(prolongator.at[s], buffer.at[s], sems.at[s])

    for s in range(sites):
        fetch(s).start()

    def turn(s, _):
        fetch(s).wait()
        out[s] = buffer[s].T
        return 0

    lax.fori_loop(0, sites, turn, 0)


def prolong_kernel(value, weights, out, buffer, sems):
    copies = []
    for s in range(value.shape[0]):
        buffer[s] = dot(value[s], weights[s]).astype(buffer.dtype)
        copies.append(pltpu.make_async_copy(buffer.at[s], out.at[s], sems.at[s]))
        copies[-1].start()
    for c in copies:
        c.wait()


def swap(count, first):
    pairs = [((i + first) % count, (i + first + 1) % count) for i in range(0, count, 2)]
    return pairs + [(b, a) for a, b in pairs]


def per_device(level2_residual, prolongator, coarse_links):
    nt, nz = lax.axis_size("ta"), lax.axis_size("gz")
    t, z = lax.axis_index("ta"), lax.axis_index("gz")
    ny, nx, rhs_count, fine = level2_residual.shape[2:]
    wide = prolongator.shape[-1]
    sites = ny * nx
    residual = level2_residual.reshape(sites, rhs_count, fine)
    prolong = prolongator.reshape(sites, fine, wide)
    links = coarse_links.reshape(9, sites, wide, wide)
    field = (sites, rhs_count, wide)
    flops = 2 * sites * rhs_count * wide * wide

    (rhs,) = call(
        restrict_kernel,
        [residual, prolong],
        [shape(field)],
        [
            pltpu.VMEM(residual.shape, residual.dtype),
            pltpu.VMEM(prolong.shape, prolong.dtype),
            pltpu.SemaphoreType.DMA((2, sites)),
        ],
        in_specs=[HBM, HBM],
    )
    t_odd, z_odd = t % 2, z % 2
    edge = (t == 0) | (t == nt - 1)
    slots = jnp.stack([8 - t_odd, 7 + t_odd, 6 - z_odd, 5 + z_odd, jnp.where(edge, -1, 1)]).astype(
        jnp.int32
    )
    local_weights, remote_weights = call(
        links_kernel,
        [slots, links],
        [shape((sites, 5 * wide, wide)), shape((sites, 4 * wide, wide))],
        [pltpu.VMEM(links.shape, links.dtype), pltpu.SemaphoreType.DMA((9,))],
        in_specs=[SMEM, HBM],
    )

    def sweep(value):
        z_near = lax.ppermute(value, "gz", swap(nz, 0))
        z_far = lax.ppermute(value, "gz", swap(nz, 1))
        t_near = lax.ppermute(value, "ta", swap(nt, 0))
        t_far = lax.ppermute(value, "ta", swap(nt, 1))
        (part,) = call(
            functools.partial(local_kernel, ny, nx),
            [rhs, value, local_weights],
            [shape(field, jnp.float32)],
            flops=5 * flops,
        )
        token = value
        for arrived in (t_far, t_near, z_far):
            (token,) = call(after_kernel, [token, arrived], [shape((8, 128), jnp.float32)])
        (value,) = call(
            remote_kernel,
            [part, t_far, t_near, z_far, z_near, remote_weights, token],
            [shape(field)],
            flops=4 * flops,
        )
        return value

    value = rhs
    for _ in range(ITERS):
        last, value = value, sweep(value)

    (weights,) = call(
        transpose_kernel,
        [prolong, last],
        [shape((sites, wide, fine))],
        [pltpu.VMEM(prolong.shape, prolong.dtype), pltpu.SemaphoreType.DMA((sites,))],
        in_specs=[HBM, VMEM],
    )
    (out,) = call(
        prolong_kernel,
        [value, weights],
        [shape((sites, rhs_count, fine))],
        [pltpu.VMEM((sites, rhs_count, fine), jnp.bfloat16), pltpu.SemaphoreType.DMA((sites,))],
        out_specs=[HBM],
    )
    return out.reshape(level2_residual.shape)


def solution(mesh):
    placed = (
        P("ta", "gz", None, None, None, None),
        P("ta", "gz", None, None, None, None),
        P(None, "ta", "gz", None, None, None, None),
    )
    return jax.shard_map(
        per_device,
        mesh=mesh,
        in_specs=placed,
        out_specs=P("ta", "gz", None, None, None, None),
        check_vma=False,
    )
```

```python
import functools

import jax
import jax.numpy as jnp
from jax import lax
from jax.experimental import pallas as pl
from jax.experimental.pallas import tpu as pltpu
from jax.sharding import PartitionSpec as P

ITERS = 16
LIMIT = 16 * 2**20
VMEM = pl.BlockSpec(memory_space=pltpu.VMEM)
HBM = pl.BlockSpec(memory_space=pltpu.HBM)
SMEM = pl.BlockSpec(memory_space=pltpu.SMEM)
NN = (((1,), (0,)), ((), ()))
NT = (((1,), (1,)), ((), ()))


def call(kernel, ins, outs, scratch=(), in_specs=None, out_specs=None, flops=0):
    in_specs = in_specs or [VMEM] * len(ins)
    out_specs = out_specs or [VMEM] * len(outs)
    ins = [
        x if spec is SMEM else pltpu.with_memory_space_constraint(x, spec.memory_space)
        for x, spec in zip(ins, in_specs)
    ]
    return pl.pallas_call(
        kernel,
        in_specs=in_specs,
        out_specs=out_specs,
        out_shape=[
            pltpu.VMEM(o.shape, o.dtype) if spec is VMEM else o for o, spec in zip(outs, out_specs)
        ],
        scratch_shapes=list(scratch),
        compiler_params=pltpu.CompilerParams(vmem_limit_bytes=LIMIT),
        cost_estimate=pl.CostEstimate(flops=flops, bytes_accessed=0, transcendentals=0),
    )(*ins)


def shape(dims, dtype=jnp.bfloat16):
    return jax.ShapeDtypeStruct(dims, dtype)


def dot(a, b, dims=NN):
    return lax.dot_general(a, b, dims, preferred_element_type=jnp.float32)


def restrict_kernel(residual, prolongator, rhs, buffer, held, sems):
    sites = rhs.shape[0]
    copies = []
    for s in range(sites):
        copies.append(
            (
                pltpu.make_async_copy(residual.at[s], buffer.at[s], sems.at[0, s]),
                pltpu.make_async_copy(prolongator.at[s], held.at[s], sems.at[1, s]),
            )
        )
        for c in copies[-1]:
            c.start()
    for s in range(sites):
        for c in copies[s]:
            c.wait()
        rhs[s] = dot(buffer[s], held[s]).astype(rhs.dtype)


def links_kernel(slots, links, remote, buffer, sems):
    sites, _, wide = remote.shape
    for i in range(4):
        pltpu.make_async_copy(links.at[slots[i]], buffer.at[i], sems.at[i]).start()
    for i in range(4):
        pltpu.make_async_copy(links.at[slots[i]], buffer.at[i], sems.at[i]).wait()
        for s in range(sites):
            remote[s, i * wide : (i + 1) * wide, :] = buffer[i, s].T

    @pl.when(slots[4] < 0)
    def _():
        remote[:, :wide, :] = -remote[:, :wide, :]


def local_kernel(ny, nx, rhs, value, links, out, buffer, sems):
    copies = []
    for y in range(ny):
        row = pl.ds(y * nx, nx)
        copies.append(pltpu.make_async_copy(links.at[:5, row], buffer.at[:, row], sems.at[y]))
        copies[-1].start()
    for y in range(ny):
        copies[y].wait()
        for x in range(nx):
            s = y * nx + x
            near = [
                s,
                y * nx + (x + 1) % nx,
                y * nx + (x - 1) % nx,
                (y + 1) % ny * nx + x,
                (y - 1) % ny * nx + x,
            ]
            lhs = jnp.concatenate([value[n] for n in near], 1)
            rows = jnp.concatenate([buffer[d, s] for d in range(5)], 1)
            out[s] = rhs[s].astype(jnp.float32) - dot(lhs, rows, NT)


def remote_kernel(part, a, b, c, d, weights, token, out):
    for s in range(part.shape[0]):
        lhs = jnp.concatenate([a[s], b[s], c[s], d[s]], 1)
        out[s] = (part[s] - dot(lhs, weights[s])).astype(out.dtype)


def after_kernel(earlier, arrived, token):
    token[...] = jnp.zeros_like(token)


def transpose_kernel(prolongator, earlier, out, buffer, sems):
    sites = out.shape[0]

    def fetch(s):
        return pltpu.make_async_copy(prolongator.at[s], buffer.at[s], sems.at[s])

    for s in range(sites):
        fetch(s).start()

    def turn(s, _):
        fetch(s).wait()
        out[s] = buffer[s].T
        return 0

    lax.fori_loop(0, sites, turn, 0)


def prolong_kernel(value, weights, out, buffer, sems):
    copies = []
    for s in range(value.shape[0]):
        buffer[s] = dot(value[s], weights[s]).astype(buffer.dtype)
        copies.append(pltpu.make_async_copy(buffer.at[s], out.at[s], sems.at[s]))
        copies[-1].start()
    for c in copies:
        c.wait()


def swap(count, first):
    pairs = [((i + first) % count, (i + first + 1) % count) for i in range(0, count, 2)]
    return pairs + [(b, a) for a, b in pairs]


def per_device(level2_residual, prolongator, coarse_links):
    nt, nz = lax.axis_size("ta"), lax.axis_size("gz")
    t, z = lax.axis_index("ta"), lax.axis_index("gz")
    ny, nx, rhs_count, fine = level2_residual.shape[2:]
    wide = prolongator.shape[-1]
    sites = ny * nx
    residual = level2_residual.reshape(sites, rhs_count, fine)
    prolong = prolongator.reshape(sites, fine, wide)
    links = coarse_links.reshape(9, sites, wide, wide)
    field = (sites, rhs_count, wide)
    flops = 2 * sites * rhs_count * wide * wide

    (rhs,) = call(
        restrict_kernel,
        [residual, prolong],
        [shape(field)],
        [
            pltpu.VMEM(residual.shape, residual.dtype),
            pltpu.VMEM(prolong.shape, prolong.dtype),
            pltpu.SemaphoreType.DMA((2, sites)),
        ],
        in_specs=[HBM, HBM],
    )
    t_odd, z_odd = t % 2, z % 2
    edge = (t == 0) | (t == nt - 1)
    slots = jnp.stack([8 - t_odd, 7 + t_odd, 6 - z_odd, 5 + z_odd, jnp.where(edge, -1, 1)]).astype(
        jnp.int32
    )
    (remote_weights,) = call(
        links_kernel,
        [slots, links],
        [shape((sites, 4 * wide, wide))],
        [pltpu.VMEM((4, *links.shape[1:]), links.dtype), pltpu.SemaphoreType.DMA((4,))],
        in_specs=[SMEM, HBM],
    )

    def sweep(value):
        z_near = lax.ppermute(value, "gz", swap(nz, 0))
        z_far = lax.ppermute(value, "gz", swap(nz, 1))
        t_near = lax.ppermute(value, "ta", swap(nt, 0))
        t_far = lax.ppermute(value, "ta", swap(nt, 1))
        (part,) = call(
            functools.partial(local_kernel, ny, nx),
            [rhs, value, links],
            [shape(field, jnp.float32)],
            [pltpu.VMEM((5, *links.shape[1:]), links.dtype), pltpu.SemaphoreType.DMA((ny,))],
            in_specs=[VMEM, VMEM, HBM],
            flops=5 * flops,
        )
        token = value
        for arrived in (t_far, t_near, z_far):
            (token,) = call(after_kernel, [token, arrived], [shape((8, 128), jnp.float32)])
        (value,) = call(
            remote_kernel,
            [part, t_far, t_near, z_far, z_near, remote_weights, token],
            [shape(field)],
            flops=4 * flops,
        )
        return value

    last = lax.fori_loop(1, ITERS - 1, lambda _, v: sweep(v), sweep(rhs))
    value = sweep(last)

    (weights,) = call(
        transpose_kernel,
        [prolong, last],
        [shape((sites, wide, fine))],
        [pltpu.VMEM(prolong.shape, prolong.dtype), pltpu.SemaphoreType.DMA((sites,))],
        in_specs=[HBM, VMEM],
    )
    (out,) = call(
        prolong_kernel,
        [value, weights],
        [shape((sites, rhs_count, fine))],
        [pltpu.VMEM((sites, rhs_count, fine), jnp.bfloat16), pltpu.SemaphoreType.DMA((sites,))],
        out_specs=[HBM],
    )
    return out.reshape(level2_residual.shape)


def solution(mesh):
    placed = (
        P("ta", "gz", None, None, None, None),
        P("ta", "gz", None, None, None, None),
        P(None, "ta", "gz", None, None, None, None),
    )
    return jax.shard_map(
        per_device,
        mesh=mesh,
        in_specs=placed,
        out_specs=P("ta", "gz", None, None, None, None),
        check_vma=False,
    )
```

```python
import functools

import jax
import jax.numpy as jnp
from jax import lax
from jax.experimental import pallas as pl
from jax.experimental.pallas import tpu as pltpu
from jax.sharding import PartitionSpec as P

ITERS = 16
LIMIT = 16 * 2**20
VMEM = pl.BlockSpec(memory_space=pltpu.VMEM)
HBM = pl.BlockSpec(memory_space=pltpu.HBM)
SMEM = pl.BlockSpec(memory_space=pltpu.SMEM)
NN = (((1,), (0,)), ((), ()))
NT = (((1,), (1,)), ((), ()))


def call(kernel, ins, outs, scratch=(), in_specs=None, out_specs=None, flops=0):
    in_specs = in_specs or [VMEM] * len(ins)
    out_specs = out_specs or [VMEM] * len(outs)
    ins = [
        x if spec is SMEM else pltpu.with_memory_space_constraint(x, spec.memory_space)
        for x, spec in zip(ins, in_specs)
    ]
    return pl.pallas_call(
        kernel,
        in_specs=in_specs,
        out_specs=out_specs,
        out_shape=[
            pltpu.VMEM(o.shape, o.dtype) if spec is VMEM else o for o, spec in zip(outs, out_specs)
        ],
        scratch_shapes=list(scratch),
        compiler_params=pltpu.CompilerParams(vmem_limit_bytes=LIMIT),
        cost_estimate=pl.CostEstimate(flops=flops, bytes_accessed=0, transcendentals=0),
    )(*ins)


def shape(dims, dtype=jnp.bfloat16):
    return jax.ShapeDtypeStruct(dims, dtype)


def dot(a, b, dims=NN):
    return lax.dot_general(a, b, dims, preferred_element_type=jnp.float32)


def restrict_kernel(residual, prolongator, rhs, buffer, held, sems):
    sites = rhs.shape[0]
    copies = []
    for s in range(sites):
        copies.append(
            (
                pltpu.make_async_copy(residual.at[s], buffer.at[s], sems.at[0, s]),
                pltpu.make_async_copy(prolongator.at[s], held.at[s], sems.at[1, s]),
            )
        )
        for c in copies[-1]:
            c.start()
    for s in range(sites):
        for c in copies[s]:
            c.wait()
        rhs[s] = dot(buffer[s], held[s]).astype(rhs.dtype)


def fetch_rows(ny, nx, links, buffer, sems):
    copies = []
    for y in range(ny):
        row = pl.ds(y * nx, nx)
        copies.append(pltpu.make_async_copy(links.at[:5, row], buffer.at[:, row], sems.at[y]))
        copies[-1].start()
    return copies


def local_rows(ny, nx, rhs, value, buffer, out, copies):
    for y in range(ny):
        copies[y].wait()
        for x in range(nx):
            s = y * nx + x
            near = [
                s,
                y * nx + (x + 1) % nx,
                y * nx + (x - 1) % nx,
                (y + 1) % ny * nx + x,
                (y - 1) % ny * nx + x,
            ]
            lhs = jnp.concatenate([value[n] for n in near], 1)
            rows = jnp.concatenate([buffer[d, s] for d in range(5)], 1)
            out[s] = rhs[s].astype(jnp.float32) - dot(lhs, rows, NT)


def local_kernel(ny, nx, rhs, value, links, out, buffer, sems):
    copies = fetch_rows(ny, nx, links, buffer, sems)
    local_rows(ny, nx, rhs, value, buffer, out, copies)


def first_kernel(ny, nx, slots, rhs, links, out, remote, buffer, sems, others, other_sems):
    sites, _, wide = remote.shape
    copies = fetch_rows(ny, nx, links, buffer, sems)

    def fetch(i):
        return pltpu.make_async_copy(links.at[slots[i]], others.at[i], other_sems.at[i])

    for i in range(4):
        fetch(i).start()
    local_rows(ny, nx, rhs, rhs, buffer, out, copies)
    for i in range(4):
        fetch(i).wait()
        for s in range(sites):
            remote[s, i * wide : (i + 1) * wide, :] = others[i, s].T

    @pl.when(slots[4] < 0)
    def _():
        remote[:, :wide, :] = -remote[:, :wide, :]


def last_kernel(ny, nx, rhs, value, links, prolongator, out, turned, buffer, sems, held, held_sems):
    copies = fetch_rows(ny, nx, links, buffer, sems)
    sites = held.shape[0]

    def fetch(s):
        return pltpu.make_async_copy(prolongator.at[s], held.at[s], held_sems.at[s])

    for s in range(sites):
        fetch(s).start()
    local_rows(ny, nx, rhs, value, buffer, out, copies)

    def turn(s, _):
        fetch(s).wait()
        turned[s] = held[s].T
        return 0

    lax.fori_loop(0, sites, turn, 0)


def remote_kernel(part, a, b, c, d, weights, token, out):
    for s in range(part.shape[0]):
        lhs = jnp.concatenate([a[s], b[s], c[s], d[s]], 1)
        out[s] = (part[s] - dot(lhs, weights[s])).astype(out.dtype)


def after_kernel(earlier, arrived, token):
    token[...] = jnp.zeros_like(token)


def prolong_kernel(value, turned, out, buffer, sems):
    copies = []
    for s in range(value.shape[0]):
        buffer[s] = dot(value[s], turned[s]).astype(buffer.dtype)
        copies.append(pltpu.make_async_copy(buffer.at[s], out.at[s], sems.at[s]))
        copies[-1].start()
    for c in copies:
        c.wait()


def swap(count, first):
    pairs = [((i + first) % count, (i + first + 1) % count) for i in range(0, count, 2)]
    return pairs + [(b, a) for a, b in pairs]


def per_device(level2_residual, prolongator, coarse_links):
    nt, nz = lax.axis_size("ta"), lax.axis_size("gz")
    t, z = lax.axis_index("ta"), lax.axis_index("gz")
    ny, nx, rhs_count, fine = level2_residual.shape[2:]
    wide = prolongator.shape[-1]
    sites = ny * nx
    residual = level2_residual.reshape(sites, rhs_count, fine)
    prolong = prolongator.reshape(sites, fine, wide)
    links = coarse_links.reshape(9, sites, wide, wide)
    field = (sites, rhs_count, wide)
    flops = 2 * sites * rhs_count * wide * wide

    (rhs,) = call(
        restrict_kernel,
        [residual, prolong],
        [shape(field)],
        [
            pltpu.VMEM(residual.shape, residual.dtype),
            pltpu.VMEM(prolong.shape, prolong.dtype),
            pltpu.SemaphoreType.DMA((2, sites)),
        ],
        in_specs=[HBM, HBM],
    )
    t_odd, z_odd = t % 2, z % 2
    edge = (t == 0) | (t == nt - 1)
    slots = jnp.stack([8 - t_odd, 7 + t_odd, 6 - z_odd, 5 + z_odd, jnp.where(edge, -1, 1)]).astype(
        jnp.int32
    )
    local_scratch = [
        pltpu.VMEM((5, *links.shape[1:]), links.dtype),
        pltpu.SemaphoreType.DMA((ny,)),
    ]

    def swaps(value):
        z_near = lax.ppermute(value, "gz", swap(nz, 0))
        z_far = lax.ppermute(value, "gz", swap(nz, 1))
        t_near = lax.ppermute(value, "ta", swap(nt, 0))
        t_far = lax.ppermute(value, "ta", swap(nt, 1))
        return t_far, t_near, z_far, z_near

    def finish(value, part, arrivals, remote_weights):
        token = value
        for arrived in arrivals[:3]:
            (token,) = call(after_kernel, [token, arrived], [shape((8, 128), jnp.float32)])
        (value,) = call(
            remote_kernel,
            [part, *arrivals, remote_weights, token],
            [shape(field)],
            flops=4 * flops,
        )
        return value

    arrivals = swaps(rhs)
    part, remote_weights = call(
        functools.partial(first_kernel, ny, nx),
        [slots, rhs, links],
        [shape(field, jnp.float32), shape((sites, 4 * wide, wide))],
        [
            *local_scratch,
            pltpu.VMEM((4, *links.shape[1:]), links.dtype),
            pltpu.SemaphoreType.DMA((4,)),
        ],
        in_specs=[SMEM, VMEM, HBM],
        flops=5 * flops,
    )
    value = finish(rhs, part, arrivals, remote_weights)

    def sweep(_, value):
        arrivals = swaps(value)
        (part,) = call(
            functools.partial(local_kernel, ny, nx),
            [rhs, value, links],
            [shape(field, jnp.float32)],
            local_scratch,
            in_specs=[VMEM, VMEM, HBM],
            flops=5 * flops,
        )
        return finish(value, part, arrivals, remote_weights)

    value = lax.fori_loop(1, ITERS - 1, sweep, value)
    arrivals = swaps(value)
    part, turned = call(
        functools.partial(last_kernel, ny, nx),
        [rhs, value, links, prolong],
        [shape(field, jnp.float32), shape((sites, wide, fine))],
        [
            *local_scratch,
            pltpu.VMEM(prolong.shape, prolong.dtype),
            pltpu.SemaphoreType.DMA((sites,)),
        ],
        in_specs=[VMEM, VMEM, HBM, HBM],
        flops=5 * flops,
    )
    value = finish(value, part, arrivals, remote_weights)

    (out,) = call(
        prolong_kernel,
        [value, turned],
        [shape((sites, rhs_count, fine))],
        [pltpu.VMEM((sites, rhs_count, fine), jnp.bfloat16), pltpu.SemaphoreType.DMA((sites,))],
        out_specs=[HBM],
    )
    return out.reshape(level2_residual.shape)


def solution(mesh):
    placed = (
        P("ta", "gz", None, None, None, None),
        P("ta", "gz", None, None, None, None),
        P(None, "ta", "gz", None, None, None, None),
    )
    return jax.shard_map(
        per_device,
        mesh=mesh,
        in_specs=placed,
        out_specs=P("ta", "gz", None, None, None, None),
        check_vma=False,
    )
```

```python
import functools

import jax
import jax.numpy as jnp
from jax import lax
from jax.experimental import pallas as pl
from jax.experimental.pallas import tpu as pltpu
from jax.sharding import PartitionSpec as P

ITERS = 16
KEPT = 1
LIMIT = 16 * 2**20
VMEM = pl.BlockSpec(memory_space=pltpu.VMEM)
HBM = pl.BlockSpec(memory_space=pltpu.HBM)
SMEM = pl.BlockSpec(memory_space=pltpu.SMEM)
NN = (((1,), (0,)), ((), ()))
NT = (((1,), (1,)), ((), ()))


def call(kernel, ins, outs, scratch=(), in_specs=None, out_specs=None, flops=0):
    in_specs = in_specs or [VMEM] * len(ins)
    out_specs = out_specs or [VMEM] * len(outs)
    ins = [
        x if spec is SMEM else pltpu.with_memory_space_constraint(x, spec.memory_space)
        for x, spec in zip(ins, in_specs)
    ]
    return pl.pallas_call(
        kernel,
        in_specs=in_specs,
        out_specs=out_specs,
        out_shape=[
            pltpu.VMEM(o.shape, o.dtype) if spec is VMEM else o for o, spec in zip(outs, out_specs)
        ],
        scratch_shapes=list(scratch),
        compiler_params=pltpu.CompilerParams(vmem_limit_bytes=LIMIT),
        cost_estimate=pl.CostEstimate(flops=flops, bytes_accessed=0, transcendentals=0),
    )(*ins)


def shape(dims, dtype=jnp.bfloat16):
    return jax.ShapeDtypeStruct(dims, dtype)


def dot(a, b, dims=NN):
    return lax.dot_general(a, b, dims, preferred_element_type=jnp.float32)


def restrict_kernel(residual, prolongator, rhs, buffer, held, sems):
    sites = rhs.shape[0]
    copies = []
    for s in range(sites):
        copies.append(
            (
                pltpu.make_async_copy(residual.at[s], buffer.at[s], sems.at[0, s]),
                pltpu.make_async_copy(prolongator.at[s], held.at[s], sems.at[1, s]),
            )
        )
        for c in copies[-1]:
            c.start()
    for first in range(0, sites, 2):
        pair = range(first, min(first + 2, sites))
        for s in pair:
            for c in copies[s]:
                c.wait()
        for s in pair:
            rhs[s] = dot(buffer[s], held[s]).astype(rhs.dtype)


def fetch_rows(ny, nx, links, buffer, sems):
    copies = []
    for y in range(ny):
        row = pl.ds(y * nx, nx)
        copies.append(pltpu.make_async_copy(links.at[KEPT:5, row], buffer.at[:, row], sems.at[y]))
        copies[-1].start()
    return copies


def local_rows(ny, nx, rhs, value, kept, buffer, out, copies):
    def near(s):
        y, x = divmod(s, nx)
        return [
            s,
            y * nx + (x + 1) % nx,
            y * nx + (x - 1) % nx,
            (y + 1) % ny * nx + x,
            (y - 1) % ny * nx + x,
        ]

    for s in range(ny * nx):
        lhs = jnp.concatenate([value[n] for n in near(s)[:KEPT]], 1)
        out[s] = rhs[s].astype(jnp.float32) - dot(lhs, kept[s])
    for y in range(ny):
        copies[y].wait()
        for s in range(y * nx, (y + 1) * nx):
            lhs = jnp.concatenate([value[n] for n in near(s)[KEPT:]], 1)
            rows = jnp.concatenate([buffer[d, s] for d in range(5 - KEPT)], 1)
            out[s] = out[s] - dot(lhs, rows, NT)


def local_kernel(ny, nx, rhs, value, kept, links, out, buffer, sems):
    copies = fetch_rows(ny, nx, links, buffer, sems)
    local_rows(ny, nx, rhs, value, kept, buffer, out, copies)


def first_kernel(ny, nx, slots, rhs, links, out, remote, kept, buffer, sems, others, other_sems):
    sites, _, wide = remote.shape
    copies = fetch_rows(ny, nx, links, buffer, sems)

    def fetch(i):
        source = slots[i] if i < 4 else i - 4
        return pltpu.make_async_copy(links.at[source], others.at[i], other_sems.at[i])

    for i in reversed(range(4 + KEPT)):
        fetch(i).start()
    for i in range(KEPT):
        fetch(4 + i).wait()
        for s in range(sites):
            kept[s, i * wide : (i + 1) * wide, :] = others[4 + i, s].T
    local_rows(ny, nx, rhs, rhs, kept, buffer, out, copies)
    for i in range(4):
        fetch(i).wait()
        for s in range(sites):
            remote[s, i * wide : (i + 1) * wide, :] = others[i, s].T

    @pl.when(slots[4] < 0)
    def _():
        remote[:, :wide, :] = -remote[:, :wide, :]


def last_kernel(ny, nx, rhs, value, kept, links, prolongator, out, turned, buffer, sems, held, held_sems):
    copies = fetch_rows(ny, nx, links, buffer, sems)
    sites = held.shape[0]

    def fetch(s):
        return pltpu.make_async_copy(prolongator.at[s], held.at[s], held_sems.at[s])

    for s in range(sites):
        fetch(s).start()
    local_rows(ny, nx, rhs, value, kept, buffer, out, copies)

    def turn(s, _):
        fetch(s).wait()
        turned[s] = held[s].T
        return 0

    lax.fori_loop(0, sites, turn, 0)


def remote_kernel(part, a, b, c, d, weights, token, out):
    for s in range(part.shape[0]):
        lhs = jnp.concatenate([a[s], b[s], c[s], d[s]], 1)
        out[s] = (part[s] - dot(lhs, weights[s])).astype(out.dtype)


def after_kernel(earlier, arrived, token):
    token[...] = jnp.zeros_like(token)


def prolong_kernel(value, turned, out, buffer, sems):
    copies = []
    for s in range(value.shape[0]):
        buffer[s] = dot(value[s], turned[s]).astype(buffer.dtype)
        copies.append(pltpu.make_async_copy(buffer.at[s], out.at[s], sems.at[s]))
        copies[-1].start()
    for c in copies:
        c.wait()


def swap(count, first):
    pairs = [((i + first) % count, (i + first + 1) % count) for i in range(0, count, 2)]
    return pairs + [(b, a) for a, b in pairs]


def per_device(level2_residual, prolongator, coarse_links):
    nt, nz = lax.axis_size("ta"), lax.axis_size("gz")
    t, z = lax.axis_index("ta"), lax.axis_index("gz")
    ny, nx, rhs_count, fine = level2_residual.shape[2:]
    wide = prolongator.shape[-1]
    sites = ny * nx
    residual = level2_residual.reshape(sites, rhs_count, fine)
    prolong = prolongator.reshape(sites, fine, wide)
    links = coarse_links.reshape(9, sites, wide, wide)
    field = (sites, rhs_count, wide)
    flops = 2 * sites * rhs_count * wide * wide

    (rhs,) = call(
        restrict_kernel,
        [residual, prolong],
        [shape(field)],
        [
            pltpu.VMEM(residual.shape, residual.dtype),
            pltpu.VMEM(prolong.shape, prolong.dtype),
            pltpu.SemaphoreType.DMA((2, sites)),
        ],
        in_specs=[HBM, HBM],
    )
    t_odd, z_odd = t % 2, z % 2
    edge = (t == 0) | (t == nt - 1)
    slots = jnp.stack([8 - t_odd, 7 + t_odd, 6 - z_odd, 5 + z_odd, jnp.where(edge, -1, 1)]).astype(
        jnp.int32
    )
    local_scratch = [
        pltpu.VMEM((5 - KEPT, *links.shape[1:]), links.dtype),
        pltpu.SemaphoreType.DMA((ny,)),
    ]

    def swaps(value):
        z_near = lax.ppermute(value, "gz", swap(nz, 0))
        z_far = lax.ppermute(value, "gz", swap(nz, 1))
        t_near = lax.ppermute(value, "ta", swap(nt, 0))
        t_far = lax.ppermute(value, "ta", swap(nt, 1))
        return t_far, t_near, z_far, z_near

    def finish(value, part, arrivals, remote_weights):
        token = value
        for arrived in arrivals[:3]:
            (token,) = call(after_kernel, [token, arrived], [shape((8, 128), jnp.float32)])
        (value,) = call(
            remote_kernel,
            [part, *arrivals, remote_weights, token],
            [shape(field)],
            flops=4 * flops,
        )
        return value

    arrivals = swaps(rhs)
    part, remote_weights, kept = call(
        functools.partial(first_kernel, ny, nx),
        [slots, rhs, links],
        [
            shape(field, jnp.float32),
            shape((sites, 4 * wide, wide)),
            shape((sites, KEPT * wide, wide)),
        ],
        [
            *local_scratch,
            pltpu.VMEM((4 + KEPT, *links.shape[1:]), links.dtype),
            pltpu.SemaphoreType.DMA((4 + KEPT,)),
        ],
        in_specs=[SMEM, VMEM, HBM],
        flops=5 * flops,
    )
    value = finish(rhs, part, arrivals, remote_weights)

    def sweep(_, value):
        arrivals = swaps(value)
        (part,) = call(
            functools.partial(local_kernel, ny, nx),
            [rhs, value, kept, links],
            [shape(field, jnp.float32)],
            local_scratch,
            in_specs=[VMEM, VMEM, VMEM, HBM],
            flops=5 * flops,
        )
        return finish(value, part, arrivals, remote_weights)

    value = lax.fori_loop(1, ITERS - 1, sweep, value)
    arrivals = swaps(value)
    part, turned = call(
        functools.partial(last_kernel, ny, nx),
        [rhs, value, kept, links, prolong],
        [shape(field, jnp.float32), shape((sites, wide, fine))],
        [
            *local_scratch,
            pltpu.VMEM(prolong.shape, prolong.dtype),
            pltpu.SemaphoreType.DMA((sites,)),
        ],
        in_specs=[VMEM, VMEM, VMEM, HBM, HBM],
        flops=5 * flops,
    )
    value = finish(value, part, arrivals, remote_weights)

    (out,) = call(
        prolong_kernel,
        [value, turned],
        [shape((sites, rhs_count, fine))],
        [pltpu.VMEM((sites, rhs_count, fine), jnp.bfloat16), pltpu.SemaphoreType.DMA((sites,))],
        out_specs=[HBM],
    )
    return out.reshape(level2_residual.shape)


def solution(mesh):
    placed = (
        P("ta", "gz", None, None, None, None),
        P("ta", "gz", None, None, None, None),
        P(None, "ta", "gz", None, None, None, None),
    )
    return jax.shard_map(
        per_device,
        mesh=mesh,
        in_specs=placed,
        out_specs=P("ta", "gz", None, None, None, None),
        check_vma=False,
    )
```

```python
import functools

import jax
import jax.numpy as jnp
from jax import lax
from jax.experimental import pallas as pl
from jax.experimental.pallas import tpu as pltpu
from jax.sharding import PartitionSpec as P

ITERS = 16
KEPT = 1
LATE = 3
LIMIT = 16 * 2**20
VMEM = pl.BlockSpec(memory_space=pltpu.VMEM)
HBM = pl.BlockSpec(memory_space=pltpu.HBM)
SMEM = pl.BlockSpec(memory_space=pltpu.SMEM)
NN = (((1,), (0,)), ((), ()))
NT = (((1,), (1,)), ((), ()))


def call(kernel, ins, outs, scratch=(), in_specs=None, out_specs=None, flops=0):
    in_specs = in_specs or [VMEM] * len(ins)
    out_specs = out_specs or [VMEM] * len(outs)
    ins = [
        x if spec is SMEM else pltpu.with_memory_space_constraint(x, spec.memory_space)
        for x, spec in zip(ins, in_specs)
    ]
    return pl.pallas_call(
        kernel,
        in_specs=in_specs,
        out_specs=out_specs,
        out_shape=[
            pltpu.VMEM(o.shape, o.dtype) if spec is VMEM else o for o, spec in zip(outs, out_specs)
        ],
        scratch_shapes=list(scratch),
        compiler_params=pltpu.CompilerParams(vmem_limit_bytes=LIMIT),
        cost_estimate=pl.CostEstimate(flops=flops, bytes_accessed=0, transcendentals=0),
    )(*ins)


def shape(dims, dtype=jnp.bfloat16):
    return jax.ShapeDtypeStruct(dims, dtype)


def dot(a, b, dims=NN):
    return lax.dot_general(a, b, dims, preferred_element_type=jnp.float32)


def restrict_kernel(residual, prolongator, rhs, buffer, held, sems):
    sites = rhs.shape[0]
    copies = []
    for s in range(sites):
        copies.append(
            (
                pltpu.make_async_copy(residual.at[s], buffer.at[s], sems.at[0, s]),
                pltpu.make_async_copy(prolongator.at[s], held.at[s], sems.at[1, s]),
            )
        )
        for c in copies[-1]:
            c.start()
    for first in range(0, sites, 2):
        pair = range(first, min(first + 2, sites))
        for s in pair:
            for c in copies[s]:
                c.wait()
        for s in pair:
            rhs[s] = dot(buffer[s], held[s]).astype(rhs.dtype)


def fetch_rows(ny, nx, links, buffer, sems):
    copies = []
    for y in range(ny):
        row = pl.ds(y * nx, nx)
        copies.append(pltpu.make_async_copy(links.at[KEPT:5, row], buffer.at[:, row], sems.at[y]))
        copies[-1].start()
    return copies


def local_rows(ny, nx, rhs, value, kept, buffer, out, copies):
    def near(s):
        y, x = divmod(s, nx)
        return [
            s,
            y * nx + (x + 1) % nx,
            y * nx + (x - 1) % nx,
            (y + 1) % ny * nx + x,
            (y - 1) % ny * nx + x,
        ]

    for s in range(ny * nx):
        lhs = jnp.concatenate([value[n] for n in near(s)[:KEPT]], 1)
        out[s] = rhs[s].astype(jnp.float32) - dot(lhs, kept[s])
    for y in range(ny):
        copies[y].wait()
        for s in range(y * nx, (y + 1) * nx):
            lhs = jnp.concatenate([value[n] for n in near(s)[KEPT:]], 1)
            rows = jnp.concatenate([buffer[d, s] for d in range(5 - KEPT)], 1)
            out[s] = out[s] - dot(lhs, rows, NT)


def local_kernel(ny, nx, rhs, value, kept, links, out, buffer, sems):
    copies = fetch_rows(ny, nx, links, buffer, sems)
    local_rows(ny, nx, rhs, value, kept, buffer, out, copies)


def first_kernel(ny, nx, slots, rhs, links, out, remote, kept, buffer, sems, others, other_sems):
    sites, _, wide = remote.shape
    copies = fetch_rows(ny, nx, links, buffer, sems)

    def fetch(i):
        source = slots[i] if i < 4 else i - 4
        return pltpu.make_async_copy(links.at[source], others.at[i], other_sems.at[i])

    for i in reversed(range(4 + KEPT)):
        fetch(i).start()
    for i in range(KEPT):
        fetch(4 + i).wait()
        for s in range(sites):
            kept[s, i * wide : (i + 1) * wide, :] = others[4 + i, s].T
    local_rows(ny, nx, rhs, rhs, kept, buffer, out, copies)
    for i in range(4):
        fetch(i).wait()
        for s in range(sites):
            remote[s, i * wide : (i + 1) * wide, :] = others[i, s].T

    @pl.when(slots[4] < 0)
    def _():
        remote[:, :wide, :] = -remote[:, :wide, :]


def last_kernel(ny, nx, first, rhs, value, kept, links, prolongator, out, turned, buffer, sems, held, held_sems):
    copies = fetch_rows(ny, nx, links, buffer, sems)
    fetched = []
    for s in range(held.shape[0]):
        fetched.append(pltpu.make_async_copy(prolongator.at[first + s], held.at[s], held_sems.at[s]))
        fetched[-1].start()
    local_rows(ny, nx, rhs, value, kept, buffer, out, copies)
    for s in range(held.shape[0]):
        fetched[s].wait()
        turned[s] = held[s].T


def remote_kernel(part, a, b, c, d, weights, token, out):
    for s in range(part.shape[0]):
        lhs = jnp.concatenate([a[s], b[s], c[s], d[s]], 1)
        out[s] = (part[s] - dot(lhs, weights[s])).astype(out.dtype)


def after_kernel(earlier, arrived, token):
    token[...] = jnp.zeros_like(token)


def prolong_kernel(value, *refs):
    *turned, out, buffer, sems = refs
    share = turned[0].shape[0]
    copies = []
    for s in range(value.shape[0]):
        weights = turned[s // share][s % share]
        buffer[s] = dot(value[s], weights).astype(buffer.dtype)
        copies.append(pltpu.make_async_copy(buffer.at[s], out.at[s], sems.at[s]))
        copies[-1].start()
    for c in copies:
        c.wait()


def swap(count, first):
    pairs = [((i + first) % count, (i + first + 1) % count) for i in range(0, count, 2)]
    return pairs + [(b, a) for a, b in pairs]


def per_device(level2_residual, prolongator, coarse_links):
    nt, nz = lax.axis_size("ta"), lax.axis_size("gz")
    t, z = lax.axis_index("ta"), lax.axis_index("gz")
    ny, nx, rhs_count, fine = level2_residual.shape[2:]
    wide = prolongator.shape[-1]
    sites = ny * nx
    residual = level2_residual.reshape(sites, rhs_count, fine)
    prolong = prolongator.reshape(sites, fine, wide)
    links = coarse_links.reshape(9, sites, wide, wide)
    field = (sites, rhs_count, wide)
    flops = 2 * sites * rhs_count * wide * wide

    (rhs,) = call(
        restrict_kernel,
        [residual, prolong],
        [shape(field)],
        [
            pltpu.VMEM(residual.shape, residual.dtype),
            pltpu.VMEM(prolong.shape, prolong.dtype),
            pltpu.SemaphoreType.DMA((2, sites)),
        ],
        in_specs=[HBM, HBM],
    )
    t_odd, z_odd = t % 2, z % 2
    edge = (t == 0) | (t == nt - 1)
    slots = jnp.stack([8 - t_odd, 7 + t_odd, 6 - z_odd, 5 + z_odd, jnp.where(edge, -1, 1)]).astype(
        jnp.int32
    )
    local_scratch = [
        pltpu.VMEM((5 - KEPT, *links.shape[1:]), links.dtype),
        pltpu.SemaphoreType.DMA((ny,)),
    ]

    def swaps(value):
        z_near = lax.ppermute(value, "gz", swap(nz, 0))
        z_far = lax.ppermute(value, "gz", swap(nz, 1))
        t_near = lax.ppermute(value, "ta", swap(nt, 0))
        t_far = lax.ppermute(value, "ta", swap(nt, 1))
        return t_far, t_near, z_far, z_near

    def finish(value, part, arrivals, remote_weights):
        token = value
        for arrived in arrivals[:3]:
            (token,) = call(after_kernel, [token, arrived], [shape((8, 128), jnp.float32)])
        (value,) = call(
            remote_kernel,
            [part, *arrivals, remote_weights, token],
            [shape(field)],
            flops=4 * flops,
        )
        return value

    arrivals = swaps(rhs)
    part, remote_weights, kept = call(
        functools.partial(first_kernel, ny, nx),
        [slots, rhs, links],
        [
            shape(field, jnp.float32),
            shape((sites, 4 * wide, wide)),
            shape((sites, KEPT * wide, wide)),
        ],
        [
            *local_scratch,
            pltpu.VMEM((4 + KEPT, *links.shape[1:]), links.dtype),
            pltpu.SemaphoreType.DMA((4 + KEPT,)),
        ],
        in_specs=[SMEM, VMEM, HBM],
        flops=5 * flops,
    )
    value = finish(rhs, part, arrivals, remote_weights)

    def sweep(_, value):
        arrivals = swaps(value)
        (part,) = call(
            functools.partial(local_kernel, ny, nx),
            [rhs, value, kept, links],
            [shape(field, jnp.float32)],
            local_scratch,
            in_specs=[VMEM, VMEM, VMEM, HBM],
            flops=5 * flops,
        )
        return finish(value, part, arrivals, remote_weights)

    value = lax.fori_loop(1, ITERS - LATE, sweep, value)
    share = sites // LATE
    turned = []
    for k in range(LATE):
        arrivals = swaps(value)
        part, some = call(
            functools.partial(last_kernel, ny, nx, k * share),
            [rhs, value, kept, links, prolong],
            [shape(field, jnp.float32), shape((share, wide, fine))],
            [
                *local_scratch,
                pltpu.VMEM((share, fine, wide), prolong.dtype),
                pltpu.SemaphoreType.DMA((share,)),
            ],
            in_specs=[VMEM, VMEM, VMEM, HBM, HBM],
            flops=5 * flops,
        )
        turned.append(some)
        value = finish(value, part, arrivals, remote_weights)

    (out,) = call(
        prolong_kernel,
        [value, *turned],
        [shape((sites, rhs_count, fine))],
        [pltpu.VMEM((sites, rhs_count, fine), jnp.bfloat16), pltpu.SemaphoreType.DMA((sites,))],
        out_specs=[HBM],
    )
    return out.reshape(level2_residual.shape)


def solution(mesh):
    placed = (
        P("ta", "gz", None, None, None, None),
        P("ta", "gz", None, None, None, None),
        P(None, "ta", "gz", None, None, None, None),
    )
    return jax.shard_map(
        per_device,
        mesh=mesh,
        in_specs=placed,
        out_specs=P("ta", "gz", None, None, None, None),
        check_vma=False,
    )
```

```python
import functools

import jax
import jax.numpy as jnp
from jax import lax
from jax.experimental import pallas as pl
from jax.experimental.pallas import tpu as pltpu
from jax.sharding import PartitionSpec as P

ITERS = 16
KEPT = 1
LATE = 4
LIMIT = 16 * 2**20
VMEM = pl.BlockSpec(memory_space=pltpu.VMEM)
HBM = pl.BlockSpec(memory_space=pltpu.HBM)
SMEM = pl.BlockSpec(memory_space=pltpu.SMEM)
NN = (((1,), (0,)), ((), ()))
NT = (((1,), (1,)), ((), ()))


def call(kernel, ins, outs, scratch=(), in_specs=None, out_specs=None, flops=0):
    in_specs = in_specs or [VMEM] * len(ins)
    out_specs = out_specs or [VMEM] * len(outs)
    ins = [
        x if spec is SMEM else pltpu.with_memory_space_constraint(x, spec.memory_space)
        for x, spec in zip(ins, in_specs)
    ]
    return pl.pallas_call(
        kernel,
        in_specs=in_specs,
        out_specs=out_specs,
        out_shape=[
            pltpu.VMEM(o.shape, o.dtype) if spec is VMEM else o for o, spec in zip(outs, out_specs)
        ],
        scratch_shapes=list(scratch),
        compiler_params=pltpu.CompilerParams(vmem_limit_bytes=LIMIT),
        cost_estimate=pl.CostEstimate(flops=flops, bytes_accessed=0, transcendentals=0),
    )(*ins)


def shape(dims, dtype=jnp.bfloat16):
    return jax.ShapeDtypeStruct(dims, dtype)


def dot(a, b, dims=NN):
    return lax.dot_general(a, b, dims, preferred_element_type=jnp.float32)


def restrict_kernel(residual, prolongator, rhs, buffer, held, sems):
    sites = rhs.shape[0]
    copies = []
    for s in range(sites):
        copies.append(
            (
                pltpu.make_async_copy(residual.at[s], buffer.at[s], sems.at[0, s]),
                pltpu.make_async_copy(prolongator.at[s], held.at[s], sems.at[1, s]),
            )
        )
        for c in copies[-1]:
            c.start()
    for first in range(0, sites, 2):
        pair = range(first, min(first + 2, sites))
        for s in pair:
            for c in copies[s]:
                c.wait()
        for s in pair:
            rhs[s] = dot(buffer[s], held[s]).astype(rhs.dtype)


def fetch_rows(ny, nx, links, buffer, sems):
    copies = []
    for y in range(ny):
        row = pl.ds(y * nx, nx)
        copies.append(pltpu.make_async_copy(links.at[KEPT:5, row], buffer.at[:, row], sems.at[y]))
        copies[-1].start()
    return copies


def local_rows(ny, nx, rhs, value, kept, buffer, out, copies):
    def near(s):
        y, x = divmod(s, nx)
        return [
            s,
            y * nx + (x + 1) % nx,
            y * nx + (x - 1) % nx,
            (y + 1) % ny * nx + x,
            (y - 1) % ny * nx + x,
        ]

    for s in range(ny * nx):
        lhs = jnp.concatenate([value[n] for n in near(s)[:KEPT]], 1)
        out[s] = rhs[s].astype(jnp.float32) - dot(lhs, kept[s])
    for y in range(ny):
        copies[y].wait()
        for s in range(y * nx, (y + 1) * nx):
            lhs = jnp.concatenate([value[n] for n in near(s)[KEPT:]], 1)
            rows = jnp.concatenate([buffer[d, s] for d in range(5 - KEPT)], 1)
            out[s] = out[s] - dot(lhs, rows, NT)


def local_kernel(ny, nx, rhs, value, kept, links, out, buffer, sems):
    copies = fetch_rows(ny, nx, links, buffer, sems)
    local_rows(ny, nx, rhs, value, kept, buffer, out, copies)


def first_kernel(ny, nx, slots, rhs, links, out, remote, kept, buffer, sems, others, other_sems):
    sites, _, wide = remote.shape
    copies = fetch_rows(ny, nx, links, buffer, sems)

    def fetch(i):
        source = slots[i] if i < 4 else i - 4
        return pltpu.make_async_copy(links.at[source], others.at[i], other_sems.at[i])

    for i in reversed(range(4 + KEPT)):
        fetch(i).start()
    for i in range(KEPT):
        fetch(4 + i).wait()
        for s in range(sites):
            kept[s, i * wide : (i + 1) * wide, :] = others[4 + i, s].T
    local_rows(ny, nx, rhs, rhs, kept, buffer, out, copies)
    for i in range(4):
        fetch(i).wait()
        for s in range(sites):
            remote[s, i * wide : (i + 1) * wide, :] = others[i, s].T

    @pl.when(slots[4] < 0)
    def _():
        remote[:, :wide, :] = -remote[:, :wide, :]


def last_kernel(ny, nx, first, rhs, value, kept, links, prolongator, out, turned, buffer, sems, held, held_sems):
    copies = fetch_rows(ny, nx, links, buffer, sems)
    fetched = []
    for s in range(held.shape[0]):
        fetched.append(pltpu.make_async_copy(prolongator.at[first + s], held.at[s], held_sems.at[s]))
        fetched[-1].start()
    local_rows(ny, nx, rhs, value, kept, buffer, out, copies)
    for s in range(held.shape[0]):
        fetched[s].wait()
        turned[s] = held[s].T


def remote_kernel(part, a, b, c, d, weights, token, out):
    for s in range(part.shape[0]):
        lhs = jnp.concatenate([a[s], b[s], c[s], d[s]], 1)
        out[s] = (part[s] - dot(lhs, weights[s])).astype(out.dtype)


def after_kernel(earlier, arrived, token):
    token[...] = jnp.zeros_like(token)


def prolong_kernel(value, *refs):
    *turned, out, buffer, sems = refs
    share = turned[0].shape[0]
    copies = []
    for s in range(value.shape[0]):
        weights = turned[s // share][s % share]
        buffer[s] = dot(value[s], weights).astype(buffer.dtype)
        copies.append(pltpu.make_async_copy(buffer.at[s], out.at[s], sems.at[s]))
        copies[-1].start()
    for c in copies:
        c.wait()


def swap(count, first):
    pairs = [((i + first) % count, (i + first + 1) % count) for i in range(0, count, 2)]
    return pairs + [(b, a) for a, b in pairs]


def per_device(level2_residual, prolongator, coarse_links):
    nt, nz = lax.axis_size("ta"), lax.axis_size("gz")
    t, z = lax.axis_index("ta"), lax.axis_index("gz")
    ny, nx, rhs_count, fine = level2_residual.shape[2:]
    wide = prolongator.shape[-1]
    sites = ny * nx
    residual = level2_residual.reshape(sites, rhs_count, fine)
    prolong = prolongator.reshape(sites, fine, wide)
    links = coarse_links.reshape(9, sites, wide, wide)
    field = (sites, rhs_count, wide)
    flops = 2 * sites * rhs_count * wide * wide

    (rhs,) = call(
        restrict_kernel,
        [residual, prolong],
        [shape(field)],
        [
            pltpu.VMEM(residual.shape, residual.dtype),
            pltpu.VMEM(prolong.shape, prolong.dtype),
            pltpu.SemaphoreType.DMA((2, sites)),
        ],
        in_specs=[HBM, HBM],
    )
    t_odd, z_odd = t % 2, z % 2
    edge = (t == 0) | (t == nt - 1)
    slots = jnp.stack([8 - t_odd, 7 + t_odd, 6 - z_odd, 5 + z_odd, jnp.where(edge, -1, 1)]).astype(
        jnp.int32
    )
    local_scratch = [
        pltpu.VMEM((5 - KEPT, *links.shape[1:]), links.dtype),
        pltpu.SemaphoreType.DMA((ny,)),
    ]

    def swaps(value):
        z_near = lax.ppermute(value, "gz", swap(nz, 0))
        z_far = lax.ppermute(value, "gz", swap(nz, 1))
        t_near = lax.ppermute(value, "ta", swap(nt, 0))
        t_far = lax.ppermute(value, "ta", swap(nt, 1))
        return t_far, t_near, z_far, z_near

    def finish(value, part, arrivals, remote_weights):
        token = value
        for arrived in arrivals[:3]:
            (token,) = call(after_kernel, [token, arrived], [shape((8, 128), jnp.float32)])
        (value,) = call(
            remote_kernel,
            [part, *arrivals, remote_weights, token],
            [shape(field)],
            flops=4 * flops,
        )
        return value

    arrivals = swaps(rhs)
    part, remote_weights, kept = call(
        functools.partial(first_kernel, ny, nx),
        [slots, rhs, links],
        [
            shape(field, jnp.float32),
            shape((sites, 4 * wide, wide)),
            shape((sites, KEPT * wide, wide)),
        ],
        [
            *local_scratch,
            pltpu.VMEM((4 + KEPT, *links.shape[1:]), links.dtype),
            pltpu.SemaphoreType.DMA((4 + KEPT,)),
        ],
        in_specs=[SMEM, VMEM, HBM],
        flops=5 * flops,
    )
    value = finish(rhs, part, arrivals, remote_weights)

    def sweep(_, value):
        arrivals = swaps(value)
        (part,) = call(
            functools.partial(local_kernel, ny, nx),
            [rhs, value, kept, links],
            [shape(field, jnp.float32)],
            local_scratch,
            in_specs=[VMEM, VMEM, VMEM, HBM],
            flops=5 * flops,
        )
        return finish(value, part, arrivals, remote_weights)

    value = lax.fori_loop(1, ITERS - LATE, sweep, value)
    share = sites // LATE
    turned = []
    for k in range(LATE):
        arrivals = swaps(value)
        part, some = call(
            functools.partial(last_kernel, ny, nx, k * share),
            [rhs, value, kept, links, prolong],
            [shape(field, jnp.float32), shape((share, wide, fine))],
            [
                *local_scratch,
                pltpu.VMEM((share, fine, wide), prolong.dtype),
                pltpu.SemaphoreType.DMA((share,)),
            ],
            in_specs=[VMEM, VMEM, VMEM, HBM, HBM],
            flops=5 * flops,
        )
        turned.append(some)
        value = finish(value, part, arrivals, remote_weights)

    (out,) = call(
        prolong_kernel,
        [value, *turned],
        [shape((sites, rhs_count, fine))],
        [pltpu.VMEM((sites, rhs_count, fine), jnp.bfloat16), pltpu.SemaphoreType.DMA((sites,))],
        out_specs=[HBM],
    )
    return out.reshape(level2_residual.shape)


def solution(mesh):
    placed = (
        P("ta", "gz", None, None, None, None),
        P("ta", "gz", None, None, None, None),
        P(None, "ta", "gz", None, None, None, None),
    )
    return jax.shard_map(
        per_device,
        mesh=mesh,
        in_specs=placed,
        out_specs=P("ta", "gz", None, None, None, None),
        check_vma=False,
    )
```

```python
import functools

import jax
import jax.numpy as jnp
from jax import lax
from jax.experimental import pallas as pl
from jax.experimental.pallas import tpu as pltpu
from jax.sharding import PartitionSpec as P

ITERS = 16
KEPT = 2
LATE = 3
LIMIT = 16 * 2**20
VMEM = pl.BlockSpec(memory_space=pltpu.VMEM)
HBM = pl.BlockSpec(memory_space=pltpu.HBM)
SMEM = pl.BlockSpec(memory_space=pltpu.SMEM)
NN = (((1,), (0,)), ((), ()))
NT = (((1,), (1,)), ((), ()))


def call(kernel, ins, outs, scratch=(), in_specs=None, out_specs=None, flops=0):
    in_specs = in_specs or [VMEM] * len(ins)
    out_specs = out_specs or [VMEM] * len(outs)
    ins = [
        x if spec is SMEM else pltpu.with_memory_space_constraint(x, spec.memory_space)
        for x, spec in zip(ins, in_specs)
    ]
    return pl.pallas_call(
        kernel,
        in_specs=in_specs,
        out_specs=out_specs,
        out_shape=[
            pltpu.VMEM(o.shape, o.dtype) if spec is VMEM else o for o, spec in zip(outs, out_specs)
        ],
        scratch_shapes=list(scratch),
        compiler_params=pltpu.CompilerParams(vmem_limit_bytes=LIMIT),
        cost_estimate=pl.CostEstimate(flops=flops, bytes_accessed=0, transcendentals=0),
    )(*ins)


def shape(dims, dtype=jnp.bfloat16):
    return jax.ShapeDtypeStruct(dims, dtype)


def dot(a, b, dims=NN):
    return lax.dot_general(a, b, dims, preferred_element_type=jnp.float32)


def restrict_kernel(residual, prolongator, rhs, buffer, held, sems):
    sites = rhs.shape[0]
    copies = []
    for s in range(sites):
        copies.append(
            (
                pltpu.make_async_copy(residual.at[s], buffer.at[s], sems.at[0, s]),
                pltpu.make_async_copy(prolongator.at[s], held.at[s], sems.at[1, s]),
            )
        )
        for c in copies[-1]:
            c.start()
    for first in range(0, sites, 2):
        pair = range(first, min(first + 2, sites))
        for s in pair:
            for c in copies[s]:
                c.wait()
        for s in pair:
            rhs[s] = dot(buffer[s], held[s]).astype(rhs.dtype)


def fetch_rows(ny, nx, links, buffer, sems):
    copies = []
    for y in range(ny):
        row = pl.ds(y * nx, nx)
        copies.append(pltpu.make_async_copy(links.at[KEPT:5, row], buffer.at[:, row], sems.at[y]))
        copies[-1].start()
    return copies


def local_rows(ny, nx, rhs, value, kept, buffer, out, copies):
    def near(s):
        y, x = divmod(s, nx)
        return [
            s,
            y * nx + (x + 1) % nx,
            y * nx + (x - 1) % nx,
            (y + 1) % ny * nx + x,
            (y - 1) % ny * nx + x,
        ]

    for s in range(ny * nx):
        lhs = jnp.concatenate([value[n] for n in near(s)[:KEPT]], 1)
        out[s] = rhs[s].astype(jnp.float32) - dot(lhs, kept[s])
    for y in range(ny):
        copies[y].wait()
        for s in range(y * nx, (y + 1) * nx):
            lhs = jnp.concatenate([value[n] for n in near(s)[KEPT:]], 1)
            rows = jnp.concatenate([buffer[d, s] for d in range(5 - KEPT)], 1)
            out[s] = out[s] - dot(lhs, rows, NT)


def local_kernel(ny, nx, rhs, value, kept, links, out, buffer, sems):
    copies = fetch_rows(ny, nx, links, buffer, sems)
    local_rows(ny, nx, rhs, value, kept, buffer, out, copies)


def first_kernel(ny, nx, slots, rhs, links, out, remote, kept, buffer, sems, others, other_sems):
    sites, _, wide = remote.shape
    copies = fetch_rows(ny, nx, links, buffer, sems)

    def fetch(i):
        source = slots[i] if i < 4 else i - 4
        return pltpu.make_async_copy(links.at[source], others.at[i], other_sems.at[i])

    for i in reversed(range(4 + KEPT)):
        fetch(i).start()
    for i in range(KEPT):
        fetch(4 + i).wait()
        for s in range(sites):
            kept[s, i * wide : (i + 1) * wide, :] = others[4 + i, s].T
    local_rows(ny, nx, rhs, rhs, kept, buffer, out, copies)
    for i in range(4):
        fetch(i).wait()
        for s in range(sites):
            remote[s, i * wide : (i + 1) * wide, :] = others[i, s].T

    @pl.when(slots[4] < 0)
    def _():
        remote[:, :wide, :] = -remote[:, :wide, :]


def last_kernel(ny, nx, first, rhs, value, kept, links, prolongator, out, turned, buffer, sems, held, held_sems):
    copies = fetch_rows(ny, nx, links, buffer, sems)
    fetched = []
    for s in range(held.shape[0]):
        fetched.append(pltpu.make_async_copy(prolongator.at[first + s], held.at[s], held_sems.at[s]))
        fetched[-1].start()
    local_rows(ny, nx, rhs, value, kept, buffer, out, copies)
    for s in range(held.shape[0]):
        fetched[s].wait()
        turned[s] = held[s].T


def remote_kernel(part, a, b, c, d, weights, token, out):
    for s in range(part.shape[0]):
        lhs = jnp.concatenate([a[s], b[s], c[s], d[s]], 1)
        out[s] = (part[s] - dot(lhs, weights[s])).astype(out.dtype)


def after_kernel(earlier, arrived, token):
    token[...] = jnp.zeros_like(token)


def prolong_kernel(value, *refs):
    *turned, out, buffer, sems = refs
    share = turned[0].shape[0]
    copies = []
    for s in range(value.shape[0]):
        weights = turned[s // share][s % share]
        buffer[s] = dot(value[s], weights).astype(buffer.dtype)
        copies.append(pltpu.make_async_copy(buffer.at[s], out.at[s], sems.at[s]))
        copies[-1].start()
    for c in copies:
        c.wait()


def swap(count, first):
    pairs = [((i + first) % count, (i + first + 1) % count) for i in range(0, count, 2)]
    return pairs + [(b, a) for a, b in pairs]


def per_device(level2_residual, prolongator, coarse_links):
    nt, nz = lax.axis_size("ta"), lax.axis_size("gz")
    t, z = lax.axis_index("ta"), lax.axis_index("gz")
    ny, nx, rhs_count, fine = level2_residual.shape[2:]
    wide = prolongator.shape[-1]
    sites = ny * nx
    residual = level2_residual.reshape(sites, rhs_count, fine)
    prolong = prolongator.reshape(sites, fine, wide)
    links = coarse_links.reshape(9, sites, wide, wide)
    field = (sites, rhs_count, wide)
    flops = 2 * sites * rhs_count * wide * wide

    (rhs,) = call(
        restrict_kernel,
        [residual, prolong],
        [shape(field)],
        [
            pltpu.VMEM(residual.shape, residual.dtype),
            pltpu.VMEM(prolong.shape, prolong.dtype),
            pltpu.SemaphoreType.DMA((2, sites)),
        ],
        in_specs=[HBM, HBM],
    )
    t_odd, z_odd = t % 2, z % 2
    edge = (t == 0) | (t == nt - 1)
    slots = jnp.stack([8 - t_odd, 7 + t_odd, 6 - z_odd, 5 + z_odd, jnp.where(edge, -1, 1)]).astype(
        jnp.int32
    )
    local_scratch = [
        pltpu.VMEM((5 - KEPT, *links.shape[1:]), links.dtype),
        pltpu.SemaphoreType.DMA((ny,)),
    ]

    def swaps(value):
        z_near = lax.ppermute(value, "gz", swap(nz, 0))
        z_far = lax.ppermute(value, "gz", swap(nz, 1))
        t_near = lax.ppermute(value, "ta", swap(nt, 0))
        t_far = lax.ppermute(value, "ta", swap(nt, 1))
        return t_far, t_near, z_far, z_near

    def finish(value, part, arrivals, remote_weights):
        token = value
        for arrived in arrivals[:3]:
            (token,) = call(after_kernel, [token, arrived], [shape((8, 128), jnp.float32)])
        (value,) = call(
            remote_kernel,
            [part, *arrivals, remote_weights, token],
            [shape(field)],
            flops=4 * flops,
        )
        return value

    arrivals = swaps(rhs)
    part, remote_weights, kept = call(
        functools.partial(first_kernel, ny, nx),
        [slots, rhs, links],
        [
            shape(field, jnp.float32),
            shape((sites, 4 * wide, wide)),
            shape((sites, KEPT * wide, wide)),
        ],
        [
            *local_scratch,
            pltpu.VMEM((4 + KEPT, *links.shape[1:]), links.dtype),
            pltpu.SemaphoreType.DMA((4 + KEPT,)),
        ],
        in_specs=[SMEM, VMEM, HBM],
        flops=5 * flops,
    )
    value = finish(rhs, part, arrivals, remote_weights)

    def sweep(_, value):
        arrivals = swaps(value)
        (part,) = call(
            functools.partial(local_kernel, ny, nx),
            [rhs, value, kept, links],
            [shape(field, jnp.float32)],
            local_scratch,
            in_specs=[VMEM, VMEM, VMEM, HBM],
            flops=5 * flops,
        )
        return finish(value, part, arrivals, remote_weights)

    value = lax.fori_loop(1, ITERS - LATE, sweep, value)
    share = sites // LATE
    turned = []
    for k in range(LATE):
        arrivals = swaps(value)
        part, some = call(
            functools.partial(last_kernel, ny, nx, k * share),
            [rhs, value, kept, links, prolong],
            [shape(field, jnp.float32), shape((share, wide, fine))],
            [
                *local_scratch,
                pltpu.VMEM((share, fine, wide), prolong.dtype),
                pltpu.SemaphoreType.DMA((share,)),
            ],
            in_specs=[VMEM, VMEM, VMEM, HBM, HBM],
            flops=5 * flops,
        )
        turned.append(some)
        value = finish(value, part, arrivals, remote_weights)

    (out,) = call(
        prolong_kernel,
        [value, *turned],
        [shape((sites, rhs_count, fine))],
        [pltpu.VMEM((sites, rhs_count, fine), jnp.bfloat16), pltpu.SemaphoreType.DMA((sites,))],
        out_specs=[HBM],
    )
    return out.reshape(level2_residual.shape)


def solution(mesh):
    placed = (
        P("ta", "gz", None, None, None, None),
        P("ta", "gz", None, None, None, None),
        P(None, "ta", "gz", None, None, None, None),
    )
    return jax.shard_map(
        per_device,
        mesh=mesh,
        in_specs=placed,
        out_specs=P("ta", "gz", None, None, None, None),
        check_vma=False,
    )
```
